512 devices in a mesh: blk: 128 (over x_lo, y, z), rep: 4 (over x_hi, core).
Axes of the slice: x: 4 (x_hi: 2, x_lo: 2; x = x_hi * 2 + x_lo), y: 4, z: 16, core: 2. Of those that a mesh axis runs over, the one named last changes fastest.
Arguments:
- user_factors: float32 [2048, 128, 256], P('blk', 'rep'), may hold values from -6 to 6
- user_state: float32 [2048, 128], P('blk', 'rep'), may hold values from 0.1 to 4
- item_factors: float32 [3, 512, 128, 256], P(None, 'blk'), may hold values from -0.375 to 0.375
- item_state: float32 [3, 512, 128], P(None, 'blk'), may hold values from 0.05 to 2
- tile_lists: int32 [2, 16384, 4], P(None, 'blk'), may hold values from 0 to 15, as said below
- tile_counts: int32 [2, 128], P(None, 'blk'), may hold values from 1 to 128, as said below
- ratings: bfloat16 [2, 16384, 128, 128], P(None, 'blk', 'rep'), may hold values from -6 to 6
Outputs:
- users_out: float32 [2048, 128, 256], P('blk', 'rep')
- user_state_out: float32 [2048, 128], P('blk', 'rep')
- items_out: float32 [3, 512, 128, 256], P(None, 'blk')
- item_state_out: float32 [3, 512, 128], P(None, 'blk')
The draws below stay inside these ranges and needn't reach their ends.
Inputs may be any that keep to these rules, and one draw needn't show every extreme that they name: `tile_lists`: column 0 is below 16, column 1 below 4, column 2 below 3, column 3 from 1 to 8. `tile_counts`: in each sub-epoch some stratum has all 128 slots live.
All inputs are finite; a program needn't handle non-finite values.
Results may differ from the reference program's by a relative error of at most 0.0032.
The reference program's roundings to bfloat16 on the way count: a program that leaves them out, or rounds other values in their place, can miss the bound.
Values sent between devices are 32-bit elements; how exact they have to be, the bound alone decides.
No kernel may reach another device: no remote copies, remote signals or barrier semaphores. Data moves between devices by JAX's collectives and lax.ppermute only.
A program may use at most 64 MiB of HBM per device.

```python
import math
import jax
import jax.numpy as jnp
from jax import lax

K = 256
TILE = 128
TASKS = 3
UT_DEV = 16
IT_DEV = 4
TMAX = 128
USER_TILES = 2048
ITEM_TILES = 512
TILES_ALL = 16384
N_BLK = 128


def draw_tile_lists(key, part):
    key = jax.random.fold_in(key, 11)
    lows = jnp.array([0, 0, 0, 1], jnp.int32)
    tops = jnp.array([UT_DEV, IT_DEV, TASKS, 9], jnp.int32)
    return jax.random.randint(key, (2, TMAX * N_BLK, 4), lows, tops, dtype=jnp.int32)


def draw_tile_counts(key, part):
    key = jax.random.fold_in(key, 12)
    first, second = jax.random.split(key)
    counts = jax.random.randint(first, (2, N_BLK), 1, TMAX // 2 + 1, dtype=jnp.int32)
    busiest = jax.random.randint(second, (2, 1), 0, N_BLK, dtype=jnp.int32)
    hit = jnp.arange(N_BLK, dtype=jnp.int32)[None, :] == busiest
    return jnp.where(hit, jnp.int32(TMAX), counts).astype(jnp.int32)


def shard_levels(own_key, shape, pieces, smallest, high):
    factor_of, own = 1.0, jax.random.fold_in(own_key, 6)
    for axis_at, parts in pieces:
        draws = jnp.exp(jax.random.uniform(jax.random.fold_in(own, axis_at), (parts,), jnp.float32, smallest / len(pieces), high / len(pieces)))
        factor_of = factor_of * jnp.repeat(draws, shape[axis_at] // parts).reshape([-1 if axis == axis_at else 1 for axis in range(len(shape))])
    return factor_of


def gaussian(own_key, extent, width, reach, shards=(), held_as=jnp.bfloat16):
    entries = jax.random.normal(own_key, extent, jnp.float32) * width
    if len(shards) > 0:
        entries = shard_levels(own_key, extent, shards, -0.22, 0.18) * entries
    return jnp.clip(entries, min=-reach, max=reach).astype(held_as)


def setup_inputs(seed: int = 0) -> dict:
    seeds = jax.random.split(jax.random.key(seed), 8)
    return {
        "user_factors": gaussian(seeds[0], (USER_TILES, TILE, K), 1.0, 6.0, ((0, 128), (1, 4)), jnp.float32),
        "user_state": jnp.clip(jnp.exp(math.log(4.0) - 3.6888794 * jax.random.uniform(seeds[1], (USER_TILES, TILE), jnp.float32) ** shard_levels(seeds[1], (USER_TILES, TILE), ((0, 128), (1, 4)), -0.2, 0.2)), 0.1, 4.0),
        "item_factors": gaussian(seeds[2], (TASKS, ITEM_TILES, TILE, K), K ** -0.5, 0.375, ((1, 128),), jnp.float32),
        "item_state": jnp.clip(jnp.exp(math.log(2.0) - 3.6888794 * jax.random.uniform(seeds[3], (TASKS, ITEM_TILES, TILE), jnp.float32) ** shard_levels(seeds[3], (TASKS, ITEM_TILES, TILE), ((1, 128),), -0.2, 0.2)), 0.05, 2.0),
        "tile_lists": draw_tile_lists(jax.random.fold_in(seeds[7], 71), 0),
        "tile_counts": draw_tile_counts(jax.random.fold_in(seeds[7], 71), 0),
        "ratings": gaussian(seeds[6], (2, TILES_ALL, TILE, TILE), 1.0, 6.0, ((1, 128), (2, 4))),
    }


decay_rate = 0.05
user_rate = 0.3
item_rate = 0.05

def adagrad(param, state, grad, rate):
    full = grad + decay_rate * param
    state_new = state + lax.optimization_barrier(jnp.mean(full * full, axis=-1))
    return (param - rate * full / jnp.sqrt(state_new)[..., None], state_new)

def stratum(users_block, items_block, lists_block, count_block, rates_block):
    tiles_user = users_block.shape[0]
    tiles_item = items_block.shape[1]
    slots = TASKS * tiles_item
    users_low = lax.optimization_barrier(users_block.astype(jnp.bfloat16)).astype(jnp.float32)
    items_low = lax.optimization_barrier(items_block.astype(jnp.bfloat16)).astype(jnp.float32)
    items_low = items_low.reshape(slots, TILE, K)
    live = jnp.arange(TMAX, dtype=jnp.int32) < count_block
    weight = jnp.where(live, lists_block[:, 3].astype(jnp.float32) * 0.25, jnp.float32(0.0))
    slot = lists_block[:, 2] * tiles_item + lists_block[:, 1]
    user_tiles = jnp.take(users_low, lists_block[:, 0], axis=0)
    item_tiles = jnp.take(items_low, slot, axis=0)
    predicted = jnp.einsum('nrk,nck->nrc', user_tiles, item_tiles, precision=lax.Precision.HIGHEST)
    error = (weight[:, None, None] * (predicted - rates_block.astype(jnp.float32))).astype(jnp.bfloat16)
    error = error.astype(jnp.float32)
    user_terms = jnp.einsum('nrc,nck->nrk', error, item_tiles, precision=lax.Precision.HIGHEST)
    item_terms = jnp.einsum('nrc,nrk->nck', error, user_tiles, precision=lax.Precision.HIGHEST)
    user_pick = (lists_block[:, 0][:, None] == jnp.arange(tiles_user, dtype=jnp.int32)[None, :]).astype(jnp.float32)
    item_pick = (slot[:, None] == jnp.arange(slots, dtype=jnp.int32)[None, :]).astype(jnp.float32)
    grad_users = jnp.einsum('nu,nrk->urk', user_pick, user_terms, precision=lax.Precision.HIGHEST)
    grad_items = jnp.einsum('ns,nck->sck', item_pick, item_terms, precision=lax.Precision.HIGHEST)
    return (grad_users, grad_items.reshape(TASKS, tiles_item, TILE, K))

def reference(user_factors, user_state, item_factors, item_state, tile_lists, tile_counts, ratings):
    users = user_factors.reshape(N_BLK, UT_DEV, TILE, K)
    ustate = user_state.reshape(N_BLK, UT_DEV, TILE)
    items = item_factors.reshape(TASKS, N_BLK, IT_DEV, TILE, K)
    istate = item_state.reshape(TASKS, N_BLK, IT_DEV, TILE)
    lists = tile_lists.reshape(2, N_BLK, TMAX, 4)
    rates = ratings.reshape(2, N_BLK, TMAX, TILE, TILE)
    for sweep in range(2):
        held = jnp.moveaxis(items, 1, 0)

        def one_block(index):
            return stratum(users[index], held[index], lists[sweep, index], tile_counts[sweep, index], rates[sweep, index])
        grad_users, grad_items = lax.map(one_block, jnp.arange(N_BLK, dtype=jnp.int32))
        users, ustate = adagrad(users, ustate, grad_users, user_rate)
        items, istate = adagrad(items, istate, jnp.moveaxis(grad_items, 0, 1), item_rate)
        if sweep == 0:
            items = jnp.roll(items, 1, axis=1)
            istate = jnp.roll(istate, 1, axis=1)
    return (users.reshape(USER_TILES, TILE, K), ustate.reshape(USER_TILES, TILE), items.reshape(TASKS, ITEM_TILES, TILE, K), istate.reshape(TASKS, ITEM_TILES, TILE))
```

```python
import functools

import jax
import jax.numpy as jnp
from jax import lax
from jax.experimental import pallas as pl
from jax.experimental.pallas import tpu as pltpu
from jax.sharding import PartitionSpec as P

decay_rate = 0.05
user_rate = 0.3
item_rate = 0.05

WIDTH = 256
TILE = 128
SLOTS = 12
HALF = SLOTS // 2
UTILES = 16
UROWS = 32
ROWS = UTILES * UROWS
CHUNKS = (6,)
OFFSETS = (0,)
UNROLL = 4
F32, BF16 = jnp.float32, jnp.bfloat16


def vmem(count):
    return [pl.BlockSpec(memory_space=pltpu.VMEM)] * count


def column_of(row):
    return jnp.broadcast_to(row, (TILE, TILE)).T[:, :1]


def row_of(column):
    return jnp.broadcast_to(column, (TILE, TILE)).T[:1, :]


def descend(param, state, grad, rate):
    full = grad + decay_rate * param
    state_new = state + jnp.mean(full * full, axis=-1, keepdims=True)
    return param - full * (rate / jnp.sqrt(state_new)), state_new


def places():
    rep = lax.axis_index("rep")
    return rep % 2, rep // 2


def grads_kernel(sweep, lists, count, ratings, users, *refs):
    n = len(CHUNKS)
    core, chip = places()
    if sweep == 0:
        items, refs = refs[0], refs[1:]
    else:
        same, cross, other, refs = refs[:n], refs[n : 2 * n], refs[2 * n : 3 * n], refs[3 * n :]
    send, keep, refs = refs[:n], refs[n : 2 * n], refs[2 * n :]
    errors, items_low, users_low, predicted, rates, users_in, *items_in, sems = refs

    copies = [
        pltpu.make_async_copy(users, users_in, sems.at[0]),
        pltpu.make_async_copy(ratings.at[sweep], rates, sems.at[1]),
    ]
    if sweep == 0:
        copies.append(pltpu.make_async_copy(items, items_in[0], sems.at[2]))
    for copy in (copies[0], *copies[2:], copies[1]):
        copy.start()
    errors[...] = jnp.zeros_like(errors)
    copies[0].wait()
    users_low[...] = users_in[...].reshape(ROWS, WIDTH).astype(BF16)
    if sweep == 0:
        copies[2].wait()
        items_low[...] = items_in[0][...].astype(BF16)
    else:
        for k in range(n):
            q = CHUNKS[k] // 2
            mine = core * HALF + OFFSETS[k]
            theirs = (1 - core) * HALF + OFFSETS[k]
            rows = q * TILE
            shape = (q, TILE, WIDTH)
            items_low[pl.ds(mine + chip * q, q)] = same[k][:rows].reshape(shape).astype(BF16)
            items_low[pl.ds(mine + (1 - chip) * q, q)] = (
                cross[k][:rows].reshape(shape).astype(BF16)
            )
            items_low[pl.ds(theirs + chip * q, q)] = other[k][:rows].reshape(shape).astype(BF16)
            items_low[pl.ds(theirs + (1 - chip) * q, q)] = (
                other[k][rows:].reshape(shape).astype(BF16)
            )

    for pair in range(SLOTS // 2):
        tiles = items_low[2 * pair : 2 * pair + 2].reshape(2 * TILE, WIDTH)
        product = lax.dot_general(
            users_low[...], tiles, (((1,), (1,)), ((), ())), preferred_element_type=F32
        )
        predicted[2 * pair] = product[:, :TILE]
        predicted[2 * pair + 1] = product[:, TILE:]
    copies[1].wait()

    live = count[0, sweep]

    def step(turn, carry):
        for lane in range(UNROLL):
            j = turn * UNROLL + lane
            row = pl.multiple_of(lists[sweep, 0, j] * UROWS, UROWS)
            slot = lists[sweep, 2, j] * 4 + lists[sweep, 1, j]
            weight = jnp.where(j < live, lists[sweep, 3, j].astype(F32) * 0.25, 0.0)
            guess = predicted[slot, pl.ds(row, UROWS), :]
            error = (weight * (guess - rates[j].astype(F32))).astype(BF16).astype(F32)
            errors[slot, pl.ds(row, UROWS), :] += error
        return carry

    lax.fori_loop(0, (live + UNROLL - 1) // UNROLL, step, 0)

    def gradient(tile):
        both = jnp.concatenate([errors[tile], errors[tile + 1]], axis=1)
        high = both.astype(BF16)
        low = (both - high.astype(F32)).astype(BF16)
        dims = (((0,), (0,)), ((), ()))
        return lax.dot_general(
            high, users_low[...], dims, preferred_element_type=F32
        ) + lax.dot_general(low, users_low[...], dims, preferred_element_type=F32)

    for k in range(n):
        for out, half in ((send[k], 1 - core), (keep[k], core)):
            for pair in range(CHUNKS[k] // 2):
                out[2 * TILE * pair : 2 * TILE * (pair + 1)] = gradient(
                    half * HALF + OFFSETS[k] + 2 * pair
                )


def users_kernel(errors, items_low, users, state, users_out, state_out):
    grad = jnp.zeros((ROWS, WIDTH), F32)
    for pair in range(SLOTS // 2):
        both = jnp.concatenate([errors[2 * pair], errors[2 * pair + 1]], axis=1)
        tiles = items_low[2 * pair : 2 * pair + 2].reshape(2 * TILE, WIDTH)
        high = both.astype(BF16)
        low = (both - high.astype(F32)).astype(BF16)
        grad += jnp.dot(high, tiles, preferred_element_type=F32)
        grad += jnp.dot(low, tiles, preferred_element_type=F32)
    lanes = lax.broadcasted_iota(jnp.int32, (UROWS, UTILES), 1)
    states = state[...].T
    out = jnp.zeros((UROWS, UTILES), F32)
    for tile in range(UTILES):
        new, column = descend(
            users[tile],
            states[:, tile : tile + 1],
            grad[tile * UROWS : (tile + 1) * UROWS],
            user_rate,
        )
        users_out[tile] = new
        out = jnp.where(lanes == tile, column, out)
    state_out[...] = out.T


def halves_kernel(after, keep, arrived, out, mine):
    del after
    core, chip = places()
    rows = out.shape[0]
    theirs = pl.ds(pl.multiple_of((1 - chip) * rows, TILE), rows)
    ours = pl.ds(pl.multiple_of(chip * rows, TILE), rows)
    out[...] = keep[theirs, :] + arrived[theirs, :]
    mine[...] = keep[ours, :] + arrived[ours, :]


def whole_kernel(after, keep, arrived, out):
    del after
    out[...] = keep[...] + arrived[...]


def first_step_kernel(tiles, mine, back, held, states, out):
    rows = tiles * TILE
    for tile in range(tiles):
        at = pl.ds(tile * TILE, TILE)
        new, column = descend(
            held[tile], column_of(states[tile : tile + 1, :]), mine[at, :] + back[at, :], item_rate
        )
        out[at, :] = new
        row = row_of(column)
        out[rows + tile : rows + tile + 1, :] = jnp.concatenate([row, row], axis=1)
    out[rows + tiles : rows + 8, :] = jnp.zeros((8 - tiles, WIDTH), F32)


def second_step_kernel(tiles, total, back, same, cross, out):
    _, chip = places()
    q = tiles // 2
    for tile in range(tiles):
        block, at = tile // q, tile % q
        source = (same, cross)[block]
        place = (chip if block == 0 else 1 - chip) * q + at
        rows = pl.ds(pl.multiple_of(place * TILE, TILE), TILE)
        new, column = descend(
            source[at * TILE : (at + 1) * TILE],
            column_of(source[q * TILE + at : q * TILE + at + 1, :TILE]),
            total[rows, :] + back[rows, :],
            item_rate,
        )
        out[tile * TILE : (tile + 1) * TILE, :] = new
        row = row_of(column)
        out[tiles * TILE + tile : tiles * TILE + tile + 1, :] = jnp.concatenate([row, row], axis=1)
    out[tiles * TILE + tiles : tiles * TILE + 8, :] = jnp.zeros((8 - tiles, WIDTH), F32)


def pack_kernel(after, same, cross, out):
    del after
    rows = out.shape[0] // 2
    out[:rows] = same[:rows]
    out[rows:] = cross[:rows]


def finish_kernel(*refs):
    n = len(CHUNKS)
    core, chip_at = places()
    own, other, (items_out, state_out) = refs[:n], refs[n : 2 * n], refs[2 * n :]
    for k in range(n):
        tiles = CHUNKS[k]
        q = tiles // 2
        for source, half in ((own[k], core), (other[k], 1 - core)):
            for tile in range(tiles):
                chip = chip_at if tile < q else 1 - chip_at
                place = half * HALF + OFFSETS[k] + chip * q + tile % q
                items_out[place] = source[tile * TILE : (tile + 1) * TILE]
                state_out[pl.ds(place, 1), :] = source[
                    tiles * TILE + tile : tiles * TILE + tile + 1, :TILE
                ]


def struct(*shape, dtype=F32):
    return jax.ShapeDtypeStruct(shape, dtype)


def call(body, name, in_specs, outs, *args, scratch=(), limit=8, work=2_000_000):
    return pl.pallas_call(
        body,
        out_shape=outs,
        in_specs=in_specs,
        out_specs=jax.tree.map(lambda _: pl.BlockSpec(memory_space=pltpu.VMEM), outs),
        scratch_shapes=scratch,
        compiler_params=pltpu.CompilerParams(vmem_limit_bytes=limit * 1024 * 1024),
        cost_estimate=pl.CostEstimate(flops=work, bytes_accessed=1_000_000, transcendentals=0),
        name=name,
    )(*args)


ANY = pl.BlockSpec(memory_space=pl.ANY)
SMEM = pl.BlockSpec(memory_space=pltpu.SMEM)


def run_grads(sweep, lists, count, ratings, users, parts):
    n = len(CHUNKS)
    shapes = [struct(t * TILE, WIDTH) for t in CHUNKS]
    scratch = [
        pltpu.VMEM((ROWS, WIDTH), BF16),
        pltpu.VMEM((SLOTS, ROWS, TILE), F32),
        pltpu.VMEM(ratings.shape[1:], BF16),
        pltpu.VMEM(users.shape, F32),
    ]
    if sweep == 0:
        scratch.append(pltpu.VMEM((SLOTS, TILE, WIDTH), F32))
    outs = call(
        functools.partial(grads_kernel, sweep),
        "grads",
        [SMEM, SMEM, ANY, ANY] + ([ANY] if sweep == 0 else vmem(len(parts))),
        shapes + shapes + [struct(SLOTS, ROWS, TILE), struct(SLOTS, TILE, WIDTH, dtype=BF16)],
        lists,
        count,
        ratings,
        users,
        *parts,
        scratch=scratch + [pltpu.SemaphoreType.DMA((3,))],
        limit=24,
        work=2_000_000_000,
    )
    return outs[:n], outs[n : 2 * n], outs[2 * n], outs[2 * n + 1]


def run_users(errors, items_low, users, state):
    return call(
        users_kernel,
        "users",
        vmem(4),
        [struct(*users.shape), struct(*state.shape)],
        errors,
        items_low,
        users,
        state,
        limit=16,
        work=1_000_000_000,
    )


def per_device(
    user_factors, user_state, item_factors, item_state, tile_lists, tile_counts, ratings
):
    n = len(CHUNKS)
    strata = lax.axis_size("blk")
    both = ("blk", "rep")
    core, chip = places()
    pairs = [(b, r) for b in range(strata) for r in range(4)]
    to_core = [(4 * b + r, 4 * b + (r ^ 1)) for b, r in pairs]
    to_chip = [(4 * b + r, 4 * b + (r ^ 2)) for b, r in pairs]
    on_same = [(4 * b + r, 4 * ((b + 1) % strata) + r) for b, r in pairs]
    on_cross = [(4 * b + r, 4 * ((b + 1) % strata) + (r ^ 2)) for b, r in pairs]

    items = item_factors.reshape(SLOTS, TILE, WIDTH)
    istate = item_state.reshape(SLOTS, TILE)
    lists = tile_lists.transpose(0, 2, 1)
    count = tile_counts.T

    send, keep, errors, low = run_grads(0, lists, count, ratings, user_factors, [items])
    arrived = [lax.ppermute(send[k], both, to_core) for k in range(n)]
    users, ustate = run_users(errors, low, user_factors, user_state)
    loads, same, cross, other = [], [], [], []
    for k in range(n):
        q = CHUNKS[k] // 2
        rows = q * TILE
        out, mine = call(
            halves_kernel,
            "halves",
            [ANY] + vmem(2),
            [struct(rows, WIDTH)] * 2,
            ustate,
            keep[k],
            arrived[k],
        )
        back = lax.ppermute(out, both, to_chip)
        tile = core * HALF + OFFSETS[k] + chip * q
        held = lax.dynamic_slice_in_dim(items, tile, q, 0)
        state = lax.dynamic_slice_in_dim(istate, tile, q, 0)
        load = call(
            functools.partial(first_step_kernel, q),
            "first_step",
            vmem(4),
            struct(rows + 8, WIDTH),
            mine,
            back,
            held,
            state,
        )
        loads.append(load)
        same.append(lax.ppermute(load, both, on_same))
        cross.append(lax.ppermute(load, both, on_cross))
    for k in range(n):
        rows = CHUNKS[k] // 2 * TILE
        whole = call(
            pack_kernel,
            "pack",
            [ANY] + vmem(2),
            struct(2 * rows, WIDTH),
            loads[-1],
            same[k],
            cross[k],
        )
        other.append(lax.ppermute(whole, both, to_core))

    send, keep, errors, low = run_grads(
        1, lists, count, ratings, users, [*same, *cross, *other]
    )
    arrived = [lax.ppermute(send[k], both, to_core) for k in range(n)]
    users, ustate = run_users(errors, low, users, ustate)
    own, rest = [], []
    for k in range(n):
        rows = CHUNKS[k] * TILE
        total = call(
            whole_kernel, "whole", [ANY] + vmem(2), struct(rows, WIDTH), ustate, keep[k], arrived[k]
        )
        back = lax.ppermute(total, both, to_chip)
        own.append(
            call(
                functools.partial(second_step_kernel, CHUNKS[k]),
                "second_step",
                vmem(4),
                struct(rows + 8, WIDTH),
                total,
                back,
                same[k],
                cross[k],
            )
        )
        rest.append(lax.ppermute(own[k], both, to_core))
    items_out, state_out = call(
        finish_kernel,
        "finish",
        vmem(2 * n),
        [struct(SLOTS, TILE, WIDTH), struct(SLOTS, TILE)],
        *own,
        *rest,
    )
    return (
        users,
        ustate,
        items_out.reshape(item_factors.shape),
        state_out.reshape(item_state.shape),
    )


def solution(mesh):
    placed = (
        P("blk", "rep", None),
        P("blk", "rep"),
        P(None, "blk", None, None),
        P(None, "blk", None),
        P(None, "blk", None),
        P(None, "blk"),
        P(None, "blk", "rep", None),
    )
    return jax.shard_map(
        per_device,
        mesh=mesh,
        in_specs=placed,
        out_specs=(
            P("blk", "rep", None),
            P("blk", "rep"),
            P(None, "blk", None, None),
            P(None, "blk", None),
        ),
        check_vma=False,
    )
```

```python
import functools

import jax
import jax.numpy as jnp
from jax import lax
from jax.experimental import pallas as pl
from jax.experimental.pallas import tpu as pltpu
from jax.sharding import PartitionSpec as P

decay_rate = 0.05
user_rate = 0.3
item_rate = 0.05

WIDTH = 256
TILE = 128
SLOTS = 12
HALF = SLOTS // 2
UTILES = 16
UROWS = 32
ROWS = UTILES * UROWS
SPLIT = 4
SHARE = HALF * TILE
UNROLL = 4
PARTS = ((0, 4), (4, 2))
RELAY_WORK = 10_000_000_000
LIMITS = (54, 24)
F32, BF16 = jnp.float32, jnp.bfloat16


def column_of(row):
    return jnp.broadcast_to(row, (TILE, TILE)).T[:, :1]


def row_of(column):
    return jnp.broadcast_to(column, (TILE, TILE)).T[:1, :]


def descend(param, state, grad, rate):
    full = grad + decay_rate * param
    state_new = state + jnp.mean(full * full, axis=-1, keepdims=True)
    return param - full * (rate / jnp.sqrt(state_new)), state_new


def places():
    rep = lax.axis_index("rep")
    return rep % 2, rep // 2


def put_state(out, row, column):
    line = row_of(column)
    out[row : row + 1, :] = jnp.concatenate([line, line], axis=1)


def grads_kernel(sweep, lists, count, ratings, users, *refs):
    core, _ = places()
    if sweep == 0:
        items, send, keep, *refs = refs
    else:
        own, other, send, keep, *refs = refs
    errors, items_low, list_in, count_in, users_low, predicted, rates, users_in, sems, *rest = refs
    leaving = []
    if sweep == 0:
        items_in, *staged, out_sems = rest
        outs = (send, keep, errors, items_low)
        send, keep, errors, items_low = staged

    def leave(which, rows=None):
        if sweep == 0:
            source, target = staged[which], outs[which]
            if rows is not None:
                source, target = source.at[rows, :], target.at[rows, :]
            copy = pltpu.make_async_copy(source, target, out_sems.at[len(leaving)])
            copy.start()
            leaving.append(copy)

    copies = [
        pltpu.make_async_copy(users, users_in, sems.at[0]),
        pltpu.make_async_copy(ratings.at[sweep], rates, sems.at[1]),
        pltpu.make_async_copy(lists.at[sweep], list_in, sems.at[2]),
        pltpu.make_async_copy(count, count_in, sems.at[3]),
    ]
    if sweep == 0:
        copies.append(pltpu.make_async_copy(items, items_in, sems.at[4]))
    for copy in (copies[0], *copies[4:], *copies[1:4]):
        copy.start()
    errors[...] = jnp.zeros_like(errors)
    copies[0].wait()
    users_low[...] = users_in[...].reshape(ROWS, WIDTH).astype(BF16)
    if sweep == 0:
        copies[4].wait()
        items_low[...] = items_in[...].astype(BF16)
    else:
        shape = (HALF, TILE, WIDTH)
        items_low[pl.ds(core * HALF, HALF)] = own[:SHARE].reshape(shape).astype(BF16)
        items_low[pl.ds((1 - core) * HALF, HALF)] = other[:SHARE].reshape(shape).astype(BF16)

    leave(3)
    for pair in range(SLOTS // 2):
        tiles = items_low[2 * pair : 2 * pair + 2].reshape(2 * TILE, WIDTH)
        product = lax.dot_general(
            users_low[...], tiles, (((1,), (1,)), ((), ())), preferred_element_type=F32
        )
        predicted[2 * pair] = product[:, :TILE]
        predicted[2 * pair + 1] = product[:, TILE:]
    for copy in copies[1:4]:
        copy.wait()

    live = count_in[0, sweep]

    def step(turn, carry):
        for lane in range(UNROLL):
            j = turn * UNROLL + lane
            row = pl.multiple_of(list_in[0, j] * UROWS, UROWS)
            slot = list_in[2, j] * 4 + list_in[1, j]
            weight = jnp.where(j < live, list_in[3, j].astype(F32) * 0.25, 0.0)
            guess = predicted[slot, pl.ds(row, UROWS), :]
            error = (weight * (guess - rates[j].astype(F32))).astype(BF16).astype(F32)
            errors[slot, pl.ds(row, UROWS), :] += error
        return carry

    lax.fori_loop(0, (live + UNROLL - 1) // UNROLL, step, 0)
    leave(2)

    def gradient(tile):
        both = jnp.concatenate([errors[tile], errors[tile + 1]], axis=1)
        high = both.astype(BF16)
        low = (both - high.astype(F32)).astype(BF16)
        dims = (((0,), (0,)), ((), ()))
        return lax.dot_general(
            high, users_low[...], dims, preferred_element_type=F32
        ) + lax.dot_general(low, users_low[...], dims, preferred_element_type=F32)

    for which, (out, half) in enumerate(((send, 1 - core), (keep, core))):
        for pair in range(HALF // 2):
            rows = pl.ds(2 * TILE * pair, 2 * TILE)
            out[rows, :] = gradient(half * HALF + 2 * pair)
            leave(which, rows)
    for copy in leaving:
        copy.wait()


def olds_kernel(keep, items, states, kept, hold, early):
    core, _ = places()
    kept[...] = keep[...]
    for out, first, tiles in ((hold, 0, SPLIT), (early, SPLIT, HALF - SPLIT)):
        rows = tiles * TILE
        base = core * HALF + first
        out[:rows] = items[pl.ds(base, tiles)].reshape(rows, WIDTH)
        for tile in range(tiles):
            place = base + tile
            line = states[place // 4, pl.ds(place % 4, 1), :]
            out[rows + tile : rows + tile + 1, :] = jnp.concatenate([line, line], axis=1)
        out[rows + tiles : rows + 8, :] = jnp.zeros((8 - tiles, WIDTH), F32)


def users_kernel(after, errors, items_low, users, state, users_out, state_out, token):
    del after
    token[...] = jnp.zeros_like(token)
    grad = jnp.zeros((ROWS, WIDTH), F32)
    for pair in range(SLOTS // 2):
        both = jnp.concatenate([errors[2 * pair], errors[2 * pair + 1]], axis=1)
        tiles = items_low[2 * pair : 2 * pair + 2].reshape(2 * TILE, WIDTH)
        high = both.astype(BF16)
        low = (both - high.astype(F32)).astype(BF16)
        grad += jnp.dot(high, tiles, preferred_element_type=F32)
        grad += jnp.dot(low, tiles, preferred_element_type=F32)
    lanes = lax.broadcasted_iota(jnp.int32, (UROWS, UTILES), 1)
    states = state[...].T
    out = jnp.zeros((UROWS, UTILES), F32)
    for tile in range(UTILES):
        new, column = descend(
            users[tile],
            states[:, tile : tile + 1],
            grad[tile * UROWS : (tile + 1) * UROWS],
            user_rate,
        )
        users_out[tile] = new
        out = jnp.where(lanes == tile, column, out)
    state_out[...] = out.T


def parts_kernel(keep, arrived, near, far):
    rows = SPLIT * TILE
    far[...] = keep[rows:] + arrived[rows:]
    near[...] = keep[:rows] + arrived[:rows]


def relay_kernel(arrived, out):
    out[...] = arrived[...]


def wholes_kernel(keep, arrived, *outs):
    for out, (first, tiles) in zip(outs, PARTS):
        rows = pl.ds(first * TILE, tiles * TILE)
        out[...] = keep[rows, :] + arrived[rows, :]


def apply_items(tiles, one, two, held, out, at, state_row, first=0):
    for tile in range(tiles):
        rows = pl.ds(tile * TILE, TILE)
        behind = held.shape[0] - 8 + first + tile
        new, column = descend(
            held[(first + tile) * TILE : (first + tile + 1) * TILE, :],
            column_of(held[behind : behind + 1, :TILE]),
            one[rows, :] + two[rows, :],
            item_rate,
        )
        out[at + tile * TILE : at + (tile + 1) * TILE, :] = new
        put_state(out, state_row + tile, column)


def step_kernel(tiles, first, one, two, held, *refs):
    out = refs[-1]
    rows = tiles * TILE
    out[rows : rows + 8, :] = jnp.zeros((8, WIDTH), F32)
    apply_items(tiles, one, two, held, out, 0, rows, first)


def join_kernel(one, two, held, done, out):
    rows = SPLIT * TILE
    out[:rows] = done[:rows]
    out[SHARE : SHARE + 8, :] = jnp.zeros((8, WIDTH), F32)
    out[SHARE : SHARE + SPLIT, :] = done[rows : rows + SPLIT, :]
    apply_items(HALF - SPLIT, one, two, held, out, rows, SHARE + SPLIT)


def place_kernel(part, *refs):
    core, _ = places()
    first, tiles = PARTS[part]
    own, other, *_, items_out, state_out, sems = refs
    rows = tiles * TILE
    copies = []
    for half, source in ((core, own), (1 - core, other)):
        start = pl.multiple_of(half * SHARE + first * TILE, TILE)
        for piece in range(2):
            copies.append(
                pltpu.make_async_copy(
                    source.at[pl.ds(piece * rows // 2, rows // 2), :],
                    items_out.at[pl.ds(start + piece * rows // 2, rows // 2), :],
                    sems.at[len(copies)],
                )
            )
            copies[-1].start()
    if part > 0:
        state_out[...] = refs[3][...]
    else:
        state_out[...] = jnp.zeros_like(state_out)
    for half, source in ((core, own), (1 - core, other)):
        for tile in range(tiles):
            place = half * HALF + first + tile
            state_out[place // 4, pl.ds(place % 4, 1), :] = source[
                rows + tile : rows + tile + 1, :TILE
            ]
    for copy in copies:
        copy.wait()


def struct(*shape, dtype=F32):
    return jax.ShapeDtypeStruct(shape, dtype)


ANY = pl.BlockSpec(memory_space=pl.ANY)
HBM = pl.BlockSpec(memory_space=pltpu.HBM)
VMEM = pl.BlockSpec(memory_space=pltpu.VMEM)


def call(body, name, in_specs, outs, *args, out_specs=None, scratch=(), limit=8,
         work=2_000_000, aliases=None):
    return pl.pallas_call(
        body,
        out_shape=outs,
        in_specs=in_specs,
        out_specs=jax.tree.map(lambda _: VMEM, outs) if out_specs is None else out_specs,
        scratch_shapes=scratch,
        input_output_aliases=aliases or {},
        compiler_params=pltpu.CompilerParams(vmem_limit_bytes=limit * 1024 * 1024),
        cost_estimate=pl.CostEstimate(flops=work, bytes_accessed=1_000_000, transcendentals=0),
        name=name,
    )(*args)


def run_grads(sweep, lists, count, ratings, users, *parts):
    share = struct(SHARE, WIDTH)
    scratch = [
        pltpu.SMEM(lists.shape[1:], jnp.int32),
        pltpu.SMEM(count.shape, jnp.int32),
        pltpu.VMEM((ROWS, WIDTH), BF16),
        pltpu.VMEM((SLOTS, ROWS, TILE), F32),
        pltpu.VMEM(ratings.shape[1:], BF16),
        pltpu.VMEM(users.shape, F32),
        pltpu.SemaphoreType.DMA((5,)),
    ]
    outs = [share, share]
    specs = [VMEM, VMEM]
    users_spec = ANY
    if sweep == 0:
        scratch += [
            pltpu.VMEM((SLOTS, TILE, WIDTH), F32),
            pltpu.VMEM((SHARE, WIDTH), F32),
            pltpu.VMEM((SHARE, WIDTH), F32),
            pltpu.VMEM((SLOTS, ROWS, TILE), F32),
            pltpu.VMEM((SLOTS, TILE, WIDTH), BF16),
            pltpu.SemaphoreType.DMA((HALF + 2,)),
        ]
        specs = [HBM]
        users_spec = HBM
    return call(
        functools.partial(grads_kernel, sweep),
        "grads",
        [HBM, HBM, HBM, users_spec] + specs,
        outs + [struct(SLOTS, ROWS, TILE), struct(SLOTS, TILE, WIDTH, dtype=BF16)],
        lists,
        count,
        ratings,
        users,
        *parts,
        out_specs=[HBM if sweep == 0 else VMEM] * 4,
        scratch=scratch,
        limit=LIMITS[sweep],
        work=2_000_000_000,
    )


def run_users(after, errors, items_low, users, state):
    return call(
        users_kernel,
        "users",
        [ANY] + [VMEM] * 4,
        [struct(*users.shape), struct(*state.shape), struct(8, TILE)],
        after,
        errors,
        items_low,
        users,
        state,
        limit=16,
        work=1_000_000_000,
    )


def per_device(
    user_factors, user_state, item_factors, item_state, tile_lists, tile_counts, ratings
):
    strata = lax.axis_size("blk")
    pairs = [(b, r) for b in range(strata) for r in range(4)]
    to_core = [(4 * b + r, 4 * b + (r ^ 1)) for b, r in pairs]
    to_chip = [(4 * b + r, 4 * b + (r ^ 2)) for b, r in pairs]
    turn = strata // 2

    def landing(b, r):
        if (b + 1) % turn == 0:
            swap = r % 2 if b + 1 == turn else 1 - r % 2
            return r ^ (2 * swap)
        return r

    to_next = [(4 * b + r, 4 * ((b + 1) % strata) + landing(b, r)) for b, r in pairs]

    def move(array, way):
        return lax.ppermute(array, ("blk", "rep"), way)

    items = item_factors.reshape(SLOTS, TILE, WIDTH)
    lists = tile_lists.transpose(0, 2, 1)
    count = tile_counts.T
    near_rows, far_rows = SPLIT * TILE, (HALF - SPLIT) * TILE

    send, keep, errors, low = run_grads(0, lists, count, ratings, user_factors, items)
    arrived = move(send, to_core)
    keep, hold, early = call(
        olds_kernel,
        "olds",
        [VMEM] * 3,
        [struct(SHARE, WIDTH), struct(near_rows + 8, WIDTH), struct(far_rows + 8, WIDTH)],
        keep,
        items,
        item_state,
    )
    old = move(early, to_next)
    near, far = call(
        parts_kernel,
        "parts",
        [VMEM] * 2,
        [struct(near_rows, WIDTH), struct(far_rows, WIDTH)],
        keep,
        arrived,
    )
    near_back = move(near, to_chip)
    far = move(far, to_next)
    far = call(relay_kernel, "relay", [VMEM], struct(far_rows, WIDTH), far, work=RELAY_WORK)
    users, ustate, _ = run_users(near, errors, low, user_factors, user_state)
    load = call(
        functools.partial(step_kernel, SPLIT, 0),
        "near_step",
        [VMEM] * 3,
        struct(near_rows + 8, WIDTH),
        near,
        near_back,
        hold,
    )
    done = move(load, to_next)
    far_back = move(far, to_chip)
    own = call(
        join_kernel, "join", [VMEM] * 4, struct(SHARE + 8, WIDTH), far, far_back, old, done
    )
    other = move(own, to_core)

    send, keep, errors, low = run_grads(1, lists, count, ratings, users, own, other)
    arrived = move(send, to_core)
    totals = call(
        wholes_kernel,
        "wholes",
        [VMEM] * 2,
        [struct(tiles * TILE, WIDTH) for _, tiles in PARTS],
        keep,
        arrived,
    )
    backs = [move(total, to_chip) for total in totals]
    users, ustate, token = run_users(totals[0], errors, low, users, ustate)
    news, others = [], []
    for (first, tiles), total, back in zip(PARTS, totals, backs):
        news.append(
            call(
                functools.partial(step_kernel, tiles, first),
                "last_step",
                [VMEM] * 3 + [ANY],
                struct(tiles * TILE + 8, WIDTH),
                total,
                back,
                own,
                token,
            )
        )
        others.append(move(news[-1], to_core))
    placed = ()
    for part in range(len(PARTS)):
        placed = call(
            functools.partial(place_kernel, part),
            "place",
            [VMEM, VMEM] + [HBM, VMEM] * (part > 0),
            [struct(2 * SHARE, WIDTH), struct(*item_state.shape)],
            news[part],
            others[part],
            *placed,
            out_specs=[HBM, VMEM],
            scratch=[pltpu.SemaphoreType.DMA((4,))],
            aliases={2: 0} if part > 0 else {},
        )
    items_out, state_out = placed
    return (users, ustate, items_out.reshape(item_factors.shape), state_out)


def solution(mesh):
    placed = (
        P("blk", "rep", None),
        P("blk", "rep"),
        P(None, "blk", None, None),
        P(None, "blk", None),
        P(None, "blk", None),
        P(None, "blk"),
        P(None, "blk", "rep", None),
    )
    return jax.shard_map(
        per_device,
        mesh=mesh,
        in_specs=placed,
        out_specs=(
            P("blk", "rep", None),
            P("blk", "rep"),
            P(None, "blk", None, None),
            P(None, "blk", None),
        ),
        check_vma=False,
    )
```
